32 devices in a mesh: groups: 2 (over x), blk: 16 (over z, y, core).
Axes of the slice: x: 2, y: 2, z: 4, core: 2. Of those that a mesh axis runs over, the one named last changes fastest.
Arguments:
- residual: bfloat16 [8, 2048, 3072], P('groups', 'blk'), parts along dimension 0, may hold values from -6 to 6
- attention: bfloat16 [8, 2048, 3072], P('groups', 'blk'), parts along dimension 0, may hold values from -6 to 6
- condition: bfloat16 [8, 3072], P('groups'), parts along dimension 0, may hold values from -4 to 4
- proj_weight: bfloat16 [3072, 3072], P('blk'), may hold values from -0.109375 to 0.109375
- mod_weight: bfloat16 [3072, 9216], P('blk'), may hold values from -0.109375 to 0.109375
- residual_cot: bfloat16 [8, 2048, 3072], P('groups', 'blk'), parts along dimension 0, may hold values from -6 to 6
- normed_cot: bfloat16 [8, 2048, 3072], P('groups', 'blk'), parts along dimension 0, may hold values from -6 to 6
Outputs:
- normed_out: bfloat16 [8, 2048, 3072], P('groups', 'blk'), parts along dimension 0
- residual_grad: bfloat16 [8, 2048, 3072], P('groups', 'blk'), parts along dimension 0
- attention_grad: bfloat16 [8, 2048, 3072], P('groups', 'blk'), parts along dimension 0
- condition_grad: float32 [8, 3072], P('groups', 'blk'), parts along dimension 0
The draws below stay inside these ranges and needn't reach their ends.
There are 2 independent parts, one for each index of `groups`. The reference program is written for one: setup_inputs(seed, part) draws one part's arguments, and reference() takes and returns one part's arrays. A program takes and returns all parts, laid end to end along the dimension named above; an argument that names none is the same for every part. Nothing has to cross between parts.
All inputs are finite; a program needn't handle non-finite values.
Results may differ from the reference program's by a relative error of at most 0.006.
Values may be sent and summed in bfloat16 or wider, within the bound.
A program may use at most 128 MiB of HBM per device.

```python
import math
import jax
import jax.numpy as jnp
from jax import lax

D = 3072
LAT = 4
SEQ = 2048


def levels(key, dims, cuts, low, largest):
    def one(dim, parts):
        draws = jax.random.uniform(jax.random.fold_in(jax.random.fold_in(key, 6), dim), (parts,), jnp.float32, low / len(cuts), largest / len(cuts))
        return jnp.repeat(jnp.exp(draws), dims[dim] // parts).reshape((-1,) + (1,) * (len(dims) - dim - 1))

    level = one(*cuts[0])
    for cut in cuts[1:]:
        level = level * one(*cut)
    return level


def centred(own_key, shape, width, limit, pieces=(), held_as=jnp.bfloat16):
    values = width * jax.random.normal(own_key, shape, jnp.float32)
    if pieces:
        values = values * levels(own_key, shape, pieces, -0.22, 0.18)
    return jnp.clip(values, -limit, limit).astype(held_as)


def setup_inputs(seed: int = 0, part: int = 0) -> dict:
    key_of = jax.random.split(jax.random.key(seed), 8)
    own_keys = jax.random.split(jax.random.fold_in(key_of[7], part), 8)
    return {
        "residual": centred(own_keys[0], (LAT, SEQ, D), 1.0, 6.0, ((1, 16),)),
        "attention": centred(own_keys[1], (LAT, SEQ, D), 1.0, 6.0, ((1, 16),)),
        "condition": centred(own_keys[2], (LAT, D), 1.0, 4.0),
        "proj_weight": centred(key_of[3], (D, D), D ** -0.5, 0.109375, ((0, 16),)),
        "mod_weight": centred(key_of[4], (D, 3 * D), D ** -0.5, 0.109375, ((0, 16),)),
        "residual_cot": centred(own_keys[5], (LAT, SEQ, D), 1.0, 6.0, ((1, 16),)),
        "normed_cot": centred(own_keys[6], (LAT, SEQ, D), 1.0, 6.0, ((1, 16),)),
    }


norm_eps = 1e-06

def silu_slope(argument):
    sigmoid_val = jax.nn.sigmoid(argument)
    return sigmoid_val * (1.0 + argument * (1.0 - sigmoid_val))

def reference(residual, attention, condition, proj_weight, mod_weight, residual_cot, normed_cot):
    condition_f32 = condition.astype(jnp.float32)
    activated = jax.nn.silu(condition_f32).astype(jnp.bfloat16)
    modulation = jnp.dot(activated, mod_weight, preferred_element_type=jnp.float32)

    def per_latent(inputs):
        res_rows, att_rows, res_cot, nrm_cot, mod_row = inputs
        gating = mod_row[None, 0:D]
        shifts = mod_row[None, D:2 * D]
        scales = mod_row[None, 2 * D:3 * D]
        projected = jnp.dot(att_rows, proj_weight, preferred_element_type=jnp.float32)
        summed = res_rows.astype(jnp.float32) + gating * projected
        average = lax.optimization_barrier(jnp.mean(summed, axis=-1, keepdims=True))
        centered = summed - average
        variance = lax.optimization_barrier(jnp.mean(centered * centered, axis=-1, keepdims=True))
        inverse = lax.rsqrt(variance + norm_eps)
        normed = centered * inverse
        normed_out = ((1.0 + scales) * normed + shifts).astype(jnp.bfloat16)
        cot_f32 = nrm_cot.astype(jnp.float32)
        normed_grad = cot_f32 * (1.0 + scales)
        summed_grad = res_cot.astype(jnp.float32) + inverse * (normed_grad - lax.optimization_barrier(jnp.mean(normed_grad, axis=-1, keepdims=True)) - normed * lax.optimization_barrier(jnp.mean(normed_grad * normed, axis=-1, keepdims=True)))
        scaled = (summed_grad * gating).astype(jnp.bfloat16)
        attn_grad = jnp.dot(scaled, proj_weight.T, preferred_element_type=jnp.float32).astype(jnp.bfloat16)
        mod_grad = jnp.concatenate([lax.optimization_barrier(jnp.sum(summed_grad * projected, axis=0)), lax.optimization_barrier(jnp.sum(cot_f32, axis=0)), lax.optimization_barrier(jnp.sum(cot_f32 * normed, axis=0))])
        return (normed_out, summed_grad.astype(jnp.bfloat16), attn_grad, mod_grad)
    normed_out, residual_grad, attention_grad, mod_grad = lax.map(per_latent, (residual, attention, residual_cot, normed_cot, modulation))
    back = jnp.dot(mod_grad, mod_weight.astype(jnp.float32).T, precision=lax.Precision.HIGHEST)
    condition_grad = silu_slope(condition_f32) * back / math.sqrt(SEQ)
    return (normed_out, residual_grad, attention_grad, condition_grad)
```

```python
import functools
import math

import jax
import jax.numpy as jnp
from jax import lax
from jax.experimental import pallas as pl
from jax.experimental.pallas import tpu as pltpu
from jax.sharding import PartitionSpec as P

norm_eps = 1e-06
MESH = pl.DeviceIdType.MESH
F32, BF16 = jnp.float32, jnp.bfloat16
HALVES = 2
COLUMN_BLOCKS = 8
TILE = 32


def kernel(
    groups, blk, latents, tokens,
    res_hbm, att_hbm, cond, w_hbm, modw_hbm, rcot_hbm, ncot_hbm,
    nout_hbm, rgrad_hbm, agrad_hbm, cgrad,
    w, att, res, rcot, ncot, modw, acc, mod, mgrad,
    stage_a, land_a, full_a, stage_b, land_b, full_b,
    load_sem, store_sem, ring_send, ring_recv, sib_send, sib_recv, own_sem,
    rs_send, rs_recv, ag_send, ag_recv,
):
    rows, features = att.shape
    shard = w_hbm.shape[0]
    chip_rows = 2 * shard
    chips = blk // 2
    third = features // 3
    piece = shard // HALVES
    steps = chips - 1
    total = steps * HALVES
    lat_rows = latents * COLUMN_BLOCKS // blk
    mod_cols = 3 * features // COLUMN_BLOCKS
    fold = groups == 2 and chips % 2 == 0

    me = lax.axis_index("blk")
    group = lax.axis_index("groups")
    core = lax.rem(me, 2)
    chip = lax.div(me, 2)
    plane = lax.rem(group, 2)

    if fold:
        side = lax.rem(chip, 2)
        along = lax.div(chip, 2)
        place = jnp.where(side == 0, along, chips - 1 - along)
    else:
        place = chip

    def chip_at(pos):
        pos = lax.rem(pos + 2 * chips, chips)
        if not fold:
            return pos
        return jnp.where(pos < chips // 2, 2 * pos, 2 * (chips - 1 - pos) + 1)

    after = {"blk": 2 * chip_at(place + 1) + core}
    before = {"blk": 2 * chip_at(place - 1) + core}
    sibling = {"blk": me + 1 - 2 * core}
    partner = {"groups": group + 1 - 2 * plane}

    cols = (
        pl.multiple_of((2 - plane) * third, third),
        0,
        pl.multiple_of((1 + plane) * third, third),
    )
    signs = (-1, 1, -1)

    loads = [
        pltpu.make_async_copy(src, dst, load_sem.at[i])
        for i, (src, dst) in enumerate(
            (
                (w_hbm, w.at[pl.ds(pl.multiple_of(me * shard, shard), shard)]),
                (modw_hbm, modw),
                (att_hbm, att),
                (ncot_hbm, ncot),
                (res_hbm, res),
                (rcot_hbm, rcot),
            )
        )
    ]
    for load in loads:
        load.start()

    barrier = pltpu.get_barrier_semaphore()

    def greet(d, carry):
        pl.semaphore_signal(
            barrier, inc=1, device_id={"blk": lax.rem(me + d, blk)}, device_id_type=MESH
        )
        return carry

    lax.fori_loop(1, blk, greet, 0)
    pl.semaphore_signal(barrier, inc=1, device_id=partner, device_id_type=MESH)
    pl.semaphore_wait(barrier, blk)

    def block(step, half, way, of_core):
        owner = chip_at(place + signs[way] * step)
        start = pl.multiple_of((2 * owner + of_core) * shard + half * piece, piece)
        return w.at[pl.ds(start, piece), pl.ds(cols[way], third)]

    def copy(ref, send, recv, device):
        return pltpu.make_async_remote_copy(
            src_ref=ref, dst_ref=ref, send_sem=send, recv_sem=recv,
            device_id=device, device_id_type=MESH,
        )

    def ring(i, way):
        device = (after, before)[way]
        step = lax.div(i, HALVES)
        return copy(
            block(step, lax.rem(i, HALVES), way, core),
            ring_send.at[way, i], ring_recv.at[way, i], device,
        )

    def arrival(i, way):
        step = lax.div(i, HALVES) + 1
        return copy(
            block(step, lax.rem(i, HALVES), way, core),
            ring_send.at[way, i], ring_recv.at[way, i], (after, before)[way],
        )

    def cross_out(i):
        step = lax.div(i, HALVES) + 1
        return copy(
            block(step, lax.rem(i, HALVES), 0, core),
            ring_send.at[2, i], ring_recv.at[2, i], partner,
        )

    def cross_in(i):
        step = lax.div(i, HALVES) + 1
        return copy(
            block(step, lax.rem(i, HALVES), 2, core),
            ring_send.at[2, i], ring_recv.at[2, i], partner,
        )

    def to_sibling(i, way, of_core):
        step = lax.div(i, HALVES) + 1
        return copy(
            block(step, lax.rem(i, HALVES), way, of_core),
            sib_send.at[way, i], sib_recv.at[way, i], sibling,
        )

    def own_to_sibling(of_core):
        start = pl.multiple_of((2 * chip + of_core) * shard, shard)
        return copy(w.at[pl.ds(start, shard)], own_sem.at[0], own_sem.at[1], sibling)

    loads[0].wait()
    for i in range(HALVES):
        ring(i, 0).start()
        ring(i, 1).start()
    own_to_sibling(core).start()

    def scatter(which, stage, land, peer, source):
        return pltpu.make_async_remote_copy(
            src_ref=stage.at[peer], dst_ref=land.at[source],
            send_sem=rs_send.at[which, peer], recv_sem=rs_recv.at[which, source],
            device_id={"blk": peer}, device_id_type=MESH,
        )

    def spread(which, full, peer, source):
        return pltpu.make_async_remote_copy(
            src_ref=full.at[source], dst_ref=full.at[source],
            send_sem=ag_send.at[which, peer], recv_sem=ag_recv.at[which, source],
            device_id={"blk": peer}, device_id_type=MESH,
        )

    def each_peer(do):
        def body(d, carry):
            do(lax.rem(me + d, blk))
            return carry

        lax.fori_loop(1, blk, body, 0)

    def sum_begin(which, values, stage, land):
        for p in range(blk):
            lat = (p // COLUMN_BLOCKS) * lat_rows
            col = (p % COLUMN_BLOCKS) * mod_cols
            stage[p] = values[lat : lat + lat_rows, col : col + mod_cols]
        each_peer(lambda peer: scatter(which, stage, land, peer, me).start())

    def sum_middle(which, stage, land, full):
        each_peer(lambda peer: scatter(which, stage, land, peer, peer).wait_recv())

        def add(d, value):
            return value + land[lax.rem(me + d, blk)]

        full[me] = lax.fori_loop(1, blk, add, stage[me])
        each_peer(lambda peer: spread(which, full, peer, me).start())

    def sum_end(which, stage, land, full, put):
        each_peer(lambda peer: spread(which, full, peer, peer).wait_recv())
        for p in range(blk):
            lat = (p // COLUMN_BLOCKS) * lat_rows
            col = (p % COLUMN_BLOCKS) * mod_cols
            for r in range(lat_rows):
                put(lat + r, col, full[p, r : r + 1, :])
        each_peer(lambda peer: scatter(which, stage, land, peer, me).wait_send())
        each_peer(lambda peer: spread(which, full, peer, me).wait_send())

    loads[1].wait()
    v = cond[...]
    act = (v * jax.nn.sigmoid(v)).astype(BF16)
    sum_begin(0, jnp.dot(act, modw[...], preferred_element_type=F32), stage_a, land_a)

    acc[...] = jnp.zeros_like(acc)
    loads[2].wait()
    overlapped = chip_rows % 128 == 0

    def multiply(step, way):
        if not overlapped:
            return
        owner = chip_at(place + signs[way] * step)
        k = pl.ds(pl.multiple_of(owner * chip_rows, chip_rows), chip_rows)
        wide = third // 2

        @pl.loop(0, 2)
        def _(n):
            c = pl.ds(pl.multiple_of(cols[way] + n * wide, wide), wide)
            acc[:, c] += jnp.dot(att[:, k], w[k, c], preferred_element_type=F32)

    def from_sibling(step, way):
        for h in range(HALVES):
            to_sibling((step - 1) * HALVES + h, way, 1 - core).wait_recv()

    def put_mod(lat, col, values):
        mod[lat, :, pl.ds(col, mod_cols)] = values

    def turn(i, carry):
        step = lax.div(i, HALVES)
        half = lax.rem(i, HALVES)
        for way in range(2):
            arrival(i, way).wait_recv()

            @pl.when(i + HALVES < total)
            def _(way=way):
                ring(i + HALVES, way).start()

            if way == 0:
                cross_out(i).start()
            to_sibling(i, way, core).start()

        @pl.when(i >= 1)
        def _():
            cross_in(i - 1).wait_recv()
            to_sibling(i - 1, 2, core).start()

        @pl.when(i == 0)
        def _():
            own_to_sibling(1 - core).wait_recv()

        @pl.when(half == 0)
        def _():
            @pl.when(step >= 1)
            def _():
                from_sibling(step, 0)
                from_sibling(step, 1)

            multiply(step, 0)
            multiply(step, 1)

        @pl.when(half == HALVES - 1)
        def _():
            @pl.when(step >= 1)
            def _():
                from_sibling(step, 2)

            multiply(step, 2)

        @pl.when(i == 1)
        def _():
            sum_middle(0, stage_a, land_a, full_a)

        @pl.when(i == 5)
        def _():
            sum_end(0, stage_a, land_a, full_a, put_mod)

        return carry

    lax.fori_loop(0, total, turn, 0)
    cross_in(total - 1).wait_recv()
    to_sibling(total - 1, 2, core).start()
    from_sibling(steps, 0)
    multiply(steps, 0)
    from_sibling(steps, 1)
    multiply(steps, 1)
    from_sibling(steps, 2)
    multiply(steps, 2)

    if not overlapped:
        @pl.loop(0, features // 256)
        def _(n):
            c = pl.ds(pl.multiple_of(n * 256, 256), 256)
            acc[:, c] = jnp.dot(att[...], w[:, c], preferred_element_type=F32)

    for load in loads[3:]:
        load.wait()
    mgrad[...] = jnp.zeros_like(mgrad)
    chunks = features // 128

    def norm(t, carry):
        lat = lax.div(t * TILE, tokens)
        r = pl.ds(pl.multiple_of(t * TILE, TILE), TILE)

        def parts(j):
            c = pl.ds(j * 128, 128)
            gate = mod[lat, :, pl.ds(j * 128, 128)]
            scale = 1.0 + mod[lat, :, pl.ds(2 * features + j * 128, 128)]
            proj = acc[r, c]
            summed = res[r, c].astype(F32) + gate * proj
            cot = ncot[r, c].astype(F32)
            return c, gate, scale, proj, summed, cot

        zero = jnp.zeros((TILE, 128), F32)
        one, two = zero, zero
        for j in range(chunks):
            _, _, scale, _, summed, cot = parts(j)
            one += summed
            two += cot * scale
        average = jnp.sum(one, axis=1, keepdims=True) / features
        grad_mean = jnp.sum(two, axis=1, keepdims=True) / features
        one, two = zero, zero
        for j in range(chunks):
            _, _, scale, _, summed, cot = parts(j)
            centered = summed - average
            one += centered * centered
            two += cot * scale * centered
        inverse = lax.rsqrt(jnp.sum(one, axis=1, keepdims=True) / features + norm_eps)
        grad_norm = inverse * (jnp.sum(two, axis=1, keepdims=True) / features)
        for j in range(chunks):
            c, gate, scale, proj, summed, cot = parts(j)
            normed = (summed - average) * inverse
            shift = mod[lat, :, pl.ds(features + j * 128, 128)]
            grad = rcot[r, c].astype(F32) + inverse * (
                cot * scale - grad_mean - normed * grad_norm
            )
            res[r, c] = (scale * normed + shift).astype(BF16)
            rcot[r, c] = grad.astype(BF16)
            att[r, c] = (grad * gate).astype(BF16)

            def fold_rows(value):
                return jnp.sum(value.reshape(TILE // 8, 8, 128), axis=0)

            for b, value in enumerate((grad * proj, cot, cot * normed)):
                mgrad[lat, :, pl.ds(b * features + j * 128, 128)] += fold_rows(value)
        return carry

    lax.fori_loop(0, rows // TILE, norm, 0)

    stores = [
        pltpu.make_async_copy(res, nout_hbm, store_sem.at[0]),
        pltpu.make_async_copy(rcot, rgrad_hbm, store_sem.at[1]),
    ]
    for store in stores:
        store.start()

    sum_begin(1, jnp.sum(mgrad[...], axis=1), stage_b, land_b)

    tiles = 8
    width = features // tiles

    def back_store(n):
        c = pl.ds(pl.multiple_of(n * width, width), width)
        return pltpu.make_async_copy(ncot.at[:, c], agrad_hbm.at[:, c], store_sem.at[2 + n])

    def back(n, carry):
        k = pl.ds(pl.multiple_of(n * width, width), width)
        ncot[:, k] = lax.dot_general(
            att[...], w[k, :], (((1,), (1,)), ((), ())), preferred_element_type=F32
        ).astype(BF16)
        back_store(n).start()

        @pl.when(n == 2)
        def _():
            sum_middle(1, stage_b, land_b, full_b)

        return carry

    lax.fori_loop(0, tiles, back, 0)

    def put_grad(lat, col, values):
        mod[lat, :, pl.ds(col, mod_cols)] = values

    sum_end(1, stage_b, land_b, full_b, put_grad)
    grads = jnp.concatenate([mod[i] for i in range(latents)], axis=0)
    upper = grads.astype(BF16).astype(F32)
    both = jnp.concatenate([upper, grads - upper], axis=0).astype(BF16)
    product = lax.dot_general(
        both, modw[...], (((1,), (1,)), ((), ())), preferred_element_type=F32
    )
    back_sum = product[:latents] + product[latents:]
    gate = jax.nn.sigmoid(v)
    slope = gate * (1.0 + v * (1.0 - gate))
    cgrad[...] = slope * back_sum / math.sqrt(tokens * blk)

    def finish(i, carry):
        ring(i, 0).wait_send()
        ring(i, 1).wait_send()
        cross_out(i).wait_send()
        for way in range(3):
            to_sibling(i, way, core).wait_send()
        return carry

    lax.fori_loop(0, total, finish, 0)
    own_to_sibling(core).wait_send()
    for store in stores:
        store.wait()

    def drain(n, carry):
        back_store(n).wait()
        return carry

    lax.fori_loop(0, tiles, drain, 0)


def local(groups, blk, residual, attention, condition, proj_weight, mod_weight, residual_cot, normed_cot):
    latents, tokens, features = residual.shape
    rows = latents * tokens
    shard = proj_weight.shape[0]
    pieces = (blk // 2 - 1) * HALVES
    own_cond = lax.dynamic_slice_in_dim(
        condition, lax.axis_index("blk") * shard, shard, 1
    ).astype(F32)
    lat_rows = latents * COLUMN_BLOCKS // blk
    mod_cols = 3 * features // COLUMN_BLOCKS
    flat = lambda a: a.reshape(rows, features)
    big = jax.ShapeDtypeStruct((rows, features), BF16)
    anywhere = pl.BlockSpec(memory_space=pl.ANY)
    vmem = pl.BlockSpec(memory_space=pltpu.VMEM)
    small = pltpu.VMEM((blk, lat_rows, mod_cols), F32)
    wide = pltpu.VMEM((rows, features), BF16)
    dma = pltpu.SemaphoreType.DMA
    outs = pl.pallas_call(
        functools.partial(kernel, groups, blk, latents, tokens),
        out_shape=(big, big, big, jax.ShapeDtypeStruct((latents, shard), F32)),
        in_specs=[anywhere, anywhere, vmem, anywhere, anywhere, anywhere, anywhere],
        out_specs=(anywhere, anywhere, anywhere, vmem),
        scratch_shapes=[
            pltpu.VMEM((shard * blk, features), BF16),
            wide, wide, wide, wide,
            pltpu.VMEM((shard, 3 * features), BF16),
            pltpu.VMEM((rows, features), F32),
            pltpu.VMEM((latents, 1, 3 * features), F32),
            pltpu.VMEM((latents, 8, 3 * features), F32),
            small, small, small, small, small, small,
            dma((6,)), dma((10,)),
            dma((3, pieces)), dma((3, pieces)), dma((3, pieces)), dma((3, pieces)),
            dma((2,)),
            dma((2, blk)), dma((2, blk)), dma((2, blk)), dma((2, blk)),
        ],
        compiler_params=pltpu.CompilerParams(
            collective_id=0, has_side_effects=True, vmem_limit_bytes=60 * 2**20
        ),
        cost_estimate=pl.CostEstimate(
            flops=4 * rows * features * features, bytes_accessed=30 * 2**20, transcendentals=0
        ),
    )(
        flat(residual), flat(attention), own_cond, proj_weight, mod_weight,
        flat(residual_cot), flat(normed_cot),
    )
    return tuple(a.reshape(latents, tokens, features) for a in outs[:3]) + (outs[3],)


def solution(mesh):
    in_specs = (
        P("groups", "blk", None),
        P("groups", "blk", None),
        P("groups", None),
        P("blk", None),
        P("blk", None),
        P("groups", "blk", None),
        P("groups", "blk", None),
    )
    out_specs = (
        P("groups", "blk", None),
        P("groups", "blk", None),
        P("groups", "blk", None),
        P("groups", "blk"),
    )
    body = functools.partial(local, mesh.shape["groups"], mesh.shape["blk"])
    return jax.shard_map(body, mesh=mesh, in_specs=in_specs, out_specs=out_specs, check_vma=False)
```

```python
import functools
import math

import jax
import jax.numpy as jnp
from jax import lax
from jax.experimental import pallas as pl
from jax.experimental.pallas import tpu as pltpu
from jax.sharding import PartitionSpec as P

norm_eps = 1e-06
MESH = pl.DeviceIdType.MESH
F32, BF16 = jnp.float32, jnp.bfloat16
HALVES = 2
COLUMN_BLOCKS = 8
TILE = 32
STORES = 4


def kernel(
    groups, blk, latents, tokens,
    res_hbm, att_hbm, cond, w_hbm, modw_hbm, rcot_hbm, ncot_hbm,
    res, rcot, ncot, grads,
    w, att, modw, acc, mod, mgrad,
    stage_a, land_a, full_a, stage_b, land_b, full_b,
    load_sem, ring_send, ring_recv, sib_send, sib_recv, own_sem,
    rs_send, rs_recv, ag_send, ag_recv,
):
    rows, features = att.shape
    shard = w_hbm.shape[0]
    chip_rows = 2 * shard
    chips = blk // 2
    third = features // 3
    piece = shard // HALVES
    steps = chips - 1
    total = steps * HALVES
    lat_rows = latents * COLUMN_BLOCKS // blk
    mod_cols = 3 * features // COLUMN_BLOCKS
    fold = groups == 2 and chips % 2 == 0

    me = lax.axis_index("blk")
    group = lax.axis_index("groups")
    core = lax.rem(me, 2)
    chip = lax.div(me, 2)
    plane = lax.rem(group, 2)

    if fold:
        side = lax.rem(chip, 2)
        along = lax.div(chip, 2)
        place = jnp.where(side == 0, along, chips - 1 - along)
    else:
        place = chip

    def chip_at(pos):
        pos = lax.rem(pos + 2 * chips, chips)
        if not fold:
            return pos
        return jnp.where(pos < chips // 2, 2 * pos, 2 * (chips - 1 - pos) + 1)

    after = {"blk": 2 * chip_at(place + 1) + core}
    before = {"blk": 2 * chip_at(place - 1) + core}
    sibling = {"blk": me + 1 - 2 * core}
    partner = {"groups": group + 1 - 2 * plane}

    cols = (
        pl.multiple_of((2 - plane) * third, third),
        0,
        pl.multiple_of((1 + plane) * third, third),
    )
    signs = (-1, 1, -1)

    loads = [
        pltpu.make_async_copy(src, dst, load_sem.at[i])
        for i, (src, dst) in enumerate(
            (
                (w_hbm, w.at[pl.ds(pl.multiple_of(me * shard, shard), shard)]),
                (modw_hbm, modw),
                (att_hbm, att),
                (ncot_hbm, ncot),
                (res_hbm, res),
                (rcot_hbm, rcot),
            )
        )
    ]
    for load in loads:
        load.start()

    barrier = pltpu.get_barrier_semaphore()

    def greet(d, carry):
        pl.semaphore_signal(
            barrier, inc=1, device_id={"blk": lax.rem(me + d, blk)}, device_id_type=MESH
        )
        return carry

    lax.fori_loop(1, blk, greet, 0)
    pl.semaphore_signal(barrier, inc=1, device_id=partner, device_id_type=MESH)
    pl.semaphore_wait(barrier, blk)

    def block(step, half, way, of_core):
        owner = chip_at(place + signs[way] * step)
        start = pl.multiple_of((2 * owner + of_core) * shard + half * piece, piece)
        return w.at[pl.ds(start, piece), pl.ds(cols[way], third)]

    def copy(ref, send, recv, device):
        return pltpu.make_async_remote_copy(
            src_ref=ref, dst_ref=ref, send_sem=send, recv_sem=recv,
            device_id=device, device_id_type=MESH,
        )

    def ring(i, way):
        device = (after, before)[way]
        step = lax.div(i, HALVES)
        return copy(
            block(step, lax.rem(i, HALVES), way, core),
            ring_send.at[way, i], ring_recv.at[way, i], device,
        )

    def arrival(i, way):
        step = lax.div(i, HALVES) + 1
        return copy(
            block(step, lax.rem(i, HALVES), way, core),
            ring_send.at[way, i], ring_recv.at[way, i], (after, before)[way],
        )

    def cross_out(i):
        step = lax.div(i, HALVES) + 1
        return copy(
            block(step, lax.rem(i, HALVES), 0, core),
            ring_send.at[2, i], ring_recv.at[2, i], partner,
        )

    def cross_in(i):
        step = lax.div(i, HALVES) + 1
        return copy(
            block(step, lax.rem(i, HALVES), 2, core),
            ring_send.at[2, i], ring_recv.at[2, i], partner,
        )

    def to_sibling(i, way, of_core):
        step = lax.div(i, HALVES) + 1
        return copy(
            block(step, lax.rem(i, HALVES), way, of_core),
            sib_send.at[way, i], sib_recv.at[way, i], sibling,
        )

    def own_to_sibling(of_core):
        start = pl.multiple_of((2 * chip + of_core) * shard, shard)
        return copy(w.at[pl.ds(start, shard)], own_sem.at[0], own_sem.at[1], sibling)

    loads[0].wait()
    for i in range(HALVES):
        ring(i, 0).start()
        ring(i, 1).start()
    own_to_sibling(core).start()

    def scatter(which, stage, land, peer, source):
        return pltpu.make_async_remote_copy(
            src_ref=stage.at[peer], dst_ref=land.at[source],
            send_sem=rs_send.at[which, peer], recv_sem=rs_recv.at[which, source],
            device_id={"blk": peer}, device_id_type=MESH,
        )

    def spread(which, full, peer, source):
        return pltpu.make_async_remote_copy(
            src_ref=full.at[source], dst_ref=full.at[source],
            send_sem=ag_send.at[which, peer], recv_sem=ag_recv.at[which, source],
            device_id={"blk": peer}, device_id_type=MESH,
        )

    def each_peer(do):
        def body(d, carry):
            do(lax.rem(me + d, blk))
            return carry

        lax.fori_loop(1, blk, body, 0)

    def sum_begin(which, values, stage, land):
        for p in range(blk):
            lat = (p // COLUMN_BLOCKS) * lat_rows
            col = (p % COLUMN_BLOCKS) * mod_cols
            stage[p] = values[lat : lat + lat_rows, col : col + mod_cols]
        each_peer(lambda peer: scatter(which, stage, land, peer, me).start())

    def sum_middle(which, stage, land, full):
        each_peer(lambda peer: scatter(which, stage, land, peer, peer).wait_recv())

        def add(d, value):
            return value + land[lax.rem(me + d, blk)]

        full[me] = lax.fori_loop(1, blk, add, stage[me])
        each_peer(lambda peer: spread(which, full, peer, me).start())

    def sum_end(which, stage, land, full, put):
        each_peer(lambda peer: spread(which, full, peer, peer).wait_recv())
        for p in range(blk):
            lat = (p // COLUMN_BLOCKS) * lat_rows
            col = (p % COLUMN_BLOCKS) * mod_cols
            for r in range(lat_rows):
                put(lat + r, col, full[p, r : r + 1, :])
        each_peer(lambda peer: scatter(which, stage, land, peer, me).wait_send())
        each_peer(lambda peer: spread(which, full, peer, me).wait_send())

    loads[1].wait()
    v = cond[...]
    act = (v * jax.nn.sigmoid(v)).astype(BF16)
    sum_begin(0, jnp.dot(act, modw[...], preferred_element_type=F32), stage_a, land_a)

    acc[...] = jnp.zeros_like(acc)
    loads[2].wait()
    overlapped = chip_rows % 128 == 0

    def multiply(step, way):
        if not overlapped:
            return
        owner = chip_at(place + signs[way] * step)
        k = pl.ds(pl.multiple_of(owner * chip_rows, chip_rows), chip_rows)
        wide = third // 2

        @pl.loop(0, 2)
        def _(n):
            c = pl.ds(pl.multiple_of(cols[way] + n * wide, wide), wide)
            acc[:, c] += jnp.dot(att[:, k], w[k, c], preferred_element_type=F32)

    def from_sibling(step, way):
        for h in range(HALVES):
            to_sibling((step - 1) * HALVES + h, way, 1 - core).wait_recv()

    def put_mod(lat, col, values):
        mod[lat, :, pl.ds(col, mod_cols)] = values

    def turn(i, carry):
        step = lax.div(i, HALVES)
        half = lax.rem(i, HALVES)
        for way in range(2):
            arrival(i, way).wait_recv()

            @pl.when(i + HALVES < total)
            def _(way=way):
                ring(i + HALVES, way).start()

            if way == 0:
                cross_out(i).start()
            to_sibling(i, way, core).start()

        @pl.when(i >= 1)
        def _():
            cross_in(i - 1).wait_recv()
            to_sibling(i - 1, 2, core).start()

        @pl.when(i == 0)
        def _():
            own_to_sibling(1 - core).wait_recv()

        @pl.when(half == 0)
        def _():
            @pl.when(step >= 1)
            def _():
                from_sibling(step, 0)
                from_sibling(step, 1)

            multiply(step, 0)
            multiply(step, 1)

        @pl.when(half == HALVES - 1)
        def _():
            @pl.when(step >= 1)
            def _():
                from_sibling(step, 2)

            multiply(step, 2)

        @pl.when(i == 1)
        def _():
            sum_middle(0, stage_a, land_a, full_a)

        @pl.when(i == 5)
        def _():
            sum_end(0, stage_a, land_a, full_a, put_mod)

        return carry

    lax.fori_loop(0, total, turn, 0)
    cross_in(total - 1).wait_recv()
    to_sibling(total - 1, 2, core).start()
    from_sibling(steps, 0)
    multiply(steps, 0)
    from_sibling(steps, 1)
    multiply(steps, 1)
    from_sibling(steps, 2)
    multiply(steps, 2)

    if not overlapped:
        @pl.loop(0, features // 256)
        def _(n):
            c = pl.ds(pl.multiple_of(n * 256, 256), 256)
            acc[:, c] = jnp.dot(att[...], w[:, c], preferred_element_type=F32)

    for load in loads[3:]:
        load.wait()
    mgrad[...] = jnp.zeros_like(mgrad)
    chunks = features // 128

    def norm(t, carry):
        lat = lax.div(t * TILE, tokens)
        r = pl.ds(pl.multiple_of(t * TILE, TILE), TILE)

        def parts(j):
            c = pl.ds(j * 128, 128)
            gate = mod[lat, :, pl.ds(j * 128, 128)]
            scale = 1.0 + mod[lat, :, pl.ds(2 * features + j * 128, 128)]
            proj = acc[r, c]
            summed = res[r, c].astype(F32) + gate * proj
            cot = ncot[r, c].astype(F32)
            return c, gate, scale, proj, summed, cot

        zero = jnp.zeros((TILE, 128), F32)
        one, two = zero, zero
        for j in range(chunks):
            _, _, scale, _, summed, cot = parts(j)
            one += summed
            two += cot * scale
        average = jnp.sum(one, axis=1, keepdims=True) / features
        grad_mean = jnp.sum(two, axis=1, keepdims=True) / features
        one, two = zero, zero
        for j in range(chunks):
            _, _, scale, _, summed, cot = parts(j)
            centered = summed - average
            one += centered * centered
            two += cot * scale * centered
        inverse = lax.rsqrt(jnp.sum(one, axis=1, keepdims=True) / features + norm_eps)
        grad_norm = inverse * (jnp.sum(two, axis=1, keepdims=True) / features)
        for j in range(chunks):
            c, gate, scale, proj, summed, cot = parts(j)
            normed = (summed - average) * inverse
            shift = mod[lat, :, pl.ds(features + j * 128, 128)]
            grad = rcot[r, c].astype(F32) + inverse * (
                cot * scale - grad_mean - normed * grad_norm
            )
            res[r, c] = (scale * normed + shift).astype(BF16)
            rcot[r, c] = grad.astype(BF16)
            att[r, c] = (grad * gate).astype(BF16)

            def fold_rows(value):
                return jnp.sum(value.reshape(TILE // 8, 8, 128), axis=0)

            for b, value in enumerate((grad * proj, cot, cot * normed)):
                mgrad[lat, :, pl.ds(b * features + j * 128, 128)] += fold_rows(value)
        return carry

    lax.fori_loop(0, rows // TILE, norm, 0)

    sum_begin(1, jnp.sum(mgrad[...], axis=1), stage_b, land_b)

    tiles = 8
    width = features // tiles

    def back(n, carry):
        k = pl.ds(pl.multiple_of(n * width, width), width)
        ncot[:, k] = lax.dot_general(
            att[...], w[k, :], (((1,), (1,)), ((), ())), preferred_element_type=F32
        ).astype(BF16)

        @pl.when(n == 2)
        def _():
            sum_middle(1, stage_b, land_b, full_b)

        return carry

    lax.fori_loop(0, tiles, back, 0)

    def put_grad(lat, col, values):
        grads[lat, :, pl.ds(col, mod_cols)] = values

    sum_end(1, stage_b, land_b, full_b, put_grad)

    def finish(i, carry):
        ring(i, 0).wait_send()
        ring(i, 1).wait_send()
        cross_out(i).wait_send()
        for way in range(3):
            to_sibling(i, way, core).wait_send()
        return carry

    lax.fori_loop(0, total, finish, 0)
    own_to_sibling(core).wait_send()

def finish_kernel(
    latents, seq_len, res, rcot, ncot, grads, cond, modw,
    nout_hbm, rgrad_hbm, agrad_hbm, cgrad, store_sem,
):
    rows = res.shape[0]
    part = rows // STORES
    stores = []
    for a, (src, dst) in enumerate(((res, nout_hbm), (rcot, rgrad_hbm), (ncot, agrad_hbm))):
        for i in range(STORES):
            r = pl.ds(i * part, part)
            stores.append(
                pltpu.make_async_copy(src.at[r], dst.at[r], store_sem.at[a * STORES + i])
            )
    for store in stores:
        store.start()
    total = jnp.concatenate([grads[i] for i in range(latents)], axis=0)
    upper = total.astype(BF16).astype(F32)
    both = jnp.concatenate([upper, total - upper], axis=0).astype(BF16)
    product = lax.dot_general(
        both, modw[...], (((1,), (1,)), ((), ())), preferred_element_type=F32
    )
    v = cond[...]
    gate = jax.nn.sigmoid(v)
    slope = gate * (1.0 + v * (1.0 - gate))
    cgrad[...] = slope * (product[:latents] + product[latents:]) / math.sqrt(seq_len)
    for store in stores:
        store.wait()


def local(groups, blk, residual, attention, condition, proj_weight, mod_weight, residual_cot, normed_cot):
    latents, tokens, features = residual.shape
    rows = latents * tokens
    shard = proj_weight.shape[0]
    pieces = (blk // 2 - 1) * HALVES
    own_cond = lax.dynamic_slice_in_dim(
        condition, lax.axis_index("blk") * shard, shard, 1
    ).astype(F32)
    lat_rows = latents * COLUMN_BLOCKS // blk
    mod_cols = 3 * features // COLUMN_BLOCKS
    flat = lambda a: a.reshape(rows, features)
    big = jax.ShapeDtypeStruct((rows, features), BF16)
    held = pltpu.VMEM((rows, features), BF16)
    anywhere = pl.BlockSpec(memory_space=pl.ANY)
    vmem = pl.BlockSpec(memory_space=pltpu.VMEM)
    small = pltpu.VMEM((blk, lat_rows, mod_cols), F32)
    wide = pltpu.VMEM((rows, features), BF16)
    dma = pltpu.SemaphoreType.DMA
    held_outs = pl.pallas_call(
        functools.partial(kernel, groups, blk, latents, tokens),
        out_shape=(held, held, held, pltpu.VMEM((latents, 1, 3 * features), F32)),
        in_specs=[anywhere, anywhere, vmem, anywhere, anywhere, anywhere, anywhere],
        out_specs=(vmem, vmem, vmem, vmem),
        scratch_shapes=[
            pltpu.VMEM((shard * blk, features), BF16),
            wide,
            pltpu.VMEM((shard, 3 * features), BF16),
            pltpu.VMEM((rows, features), F32),
            pltpu.VMEM((latents, 1, 3 * features), F32),
            pltpu.VMEM((latents, 8, 3 * features), F32),
            small, small, small, small, small, small,
            dma((6,)),
            dma((3, pieces)), dma((3, pieces)), dma((3, pieces)), dma((3, pieces)),
            dma((2,)),
            dma((2, blk)), dma((2, blk)), dma((2, blk)), dma((2, blk)),
        ],
        compiler_params=pltpu.CompilerParams(
            collective_id=0, has_side_effects=True, vmem_limit_bytes=48 * 2**20
        ),
        cost_estimate=pl.CostEstimate(
            flops=4 * rows * features * features, bytes_accessed=30 * 2**20, transcendentals=0
        ),
    )(
        flat(residual), flat(attention), own_cond, proj_weight, mod_weight,
        flat(residual_cot), flat(normed_cot),
    )
    outs = pl.pallas_call(
        functools.partial(finish_kernel, latents, tokens * blk),
        out_shape=(big, big, big, jax.ShapeDtypeStruct((latents, shard), F32)),
        in_specs=[vmem] * 6,
        out_specs=(anywhere, anywhere, anywhere, vmem),
        scratch_shapes=[dma((3 * STORES,))],
        compiler_params=pltpu.CompilerParams(vmem_limit_bytes=16 * 2**20),
    )(*held_outs, own_cond, mod_weight)
    return tuple(a.reshape(latents, tokens, features) for a in outs[:3]) + (outs[3],)


def solution(mesh):
    in_specs = (
        P("groups", "blk", None),
        P("groups", "blk", None),
        P("groups", None),
        P("blk", None),
        P("blk", None),
        P("groups", "blk", None),
        P("groups", "blk", None),
    )
    out_specs = (
        P("groups", "blk", None),
        P("groups", "blk", None),
        P("groups", "blk", None),
        P("groups", "blk"),
    )
    body = functools.partial(local, mesh.shape["groups"], mesh.shape["blk"])
    return jax.shard_map(body, mesh=mesh, in_specs=in_specs, out_specs=out_specs, check_vma=False)
```

```python
import functools
import math

import jax
import jax.numpy as jnp
from jax import lax
from jax.experimental import pallas as pl
from jax.experimental.pallas import tpu as pltpu
from jax.sharding import PartitionSpec as P

norm_eps = 1e-06
MESH = pl.DeviceIdType.MESH
F32, BF16 = jnp.float32, jnp.bfloat16
HALVES = 2
COLUMN_BLOCKS = 8
TILE = 32
STORES = 4


def kernel(
    groups, blk, latents, tokens,
    res_hbm, att_hbm, cond, w_hbm, modw_hbm, rcot_hbm, ncot_hbm,
    res, rcot, ncot, grads, own,
    w, att, modw, acc, mod, mgrad,
    stage_a, land_a, full_a, stage_b, land_b, full_b,
    load_sem, ring_send, ring_recv, sib_send, sib_recv, own_sem,
    rs_send, rs_recv, ag_send, ag_recv,
):
    rows, features = att.shape
    shard = w_hbm.shape[0]
    chip_rows = 2 * shard
    chips = blk // 2
    overlapped = chip_rows % 128 == 0
    third = features // 3
    piece = shard // HALVES
    steps = chips - 1
    total = steps * HALVES
    lat_rows = latents * COLUMN_BLOCKS // blk
    mod_cols = 3 * features // COLUMN_BLOCKS
    fold = groups == 2 and chips % 2 == 0

    me = lax.axis_index("blk")
    group = lax.axis_index("groups")
    core = lax.rem(me, 2)
    chip = lax.div(me, 2)
    plane = lax.rem(group, 2)

    if fold:
        side = lax.rem(chip, 2)
        along = lax.div(chip, 2)
        place = jnp.where(side == 0, along, chips - 1 - along)
    else:
        place = chip

    def chip_at(pos):
        pos = lax.rem(pos + 2 * chips, chips)
        if not fold:
            return pos
        return jnp.where(pos < chips // 2, 2 * pos, 2 * (chips - 1 - pos) + 1)

    after = {"blk": 2 * chip_at(place + 1) + core}
    before = {"blk": 2 * chip_at(place - 1) + core}
    sibling = {"blk": me + 1 - 2 * core}
    partner = {"groups": group + 1 - 2 * plane}

    cols = (
        pl.multiple_of((2 - plane) * third, third),
        0,
        pl.multiple_of((1 + plane) * third, third),
    )
    signs = (-1, 1, -1)

    loads = [
        pltpu.make_async_copy(src, dst, load_sem.at[i])
        for i, (src, dst) in enumerate(
            (
                (w_hbm, w.at[pl.ds(pl.multiple_of(me * shard, shard), shard)]),
                (modw_hbm, modw),
                (att_hbm, att),
                (ncot_hbm, ncot),
                (res_hbm, res),
                (rcot_hbm, rcot),
            )
        )
    ]
    for load in loads:
        load.start()

    barrier = pltpu.get_barrier_semaphore()

    def greet(d, carry):
        pl.semaphore_signal(
            barrier, inc=1, device_id={"blk": lax.rem(me + d, blk)}, device_id_type=MESH
        )
        return carry

    lax.fori_loop(1, blk, greet, 0)
    pl.semaphore_signal(barrier, inc=1, device_id=partner, device_id_type=MESH)
    pl.semaphore_wait(barrier, blk)

    def block(step, half, way, of_core):
        owner = chip_at(place + signs[way] * step)
        start = pl.multiple_of((2 * owner + of_core) * shard + half * piece, piece)
        return w.at[pl.ds(start, piece), pl.ds(cols[way], third)]

    def copy(ref, send, recv, device):
        return pltpu.make_async_remote_copy(
            src_ref=ref, dst_ref=ref, send_sem=send, recv_sem=recv,
            device_id=device, device_id_type=MESH,
        )

    def ring(i, way):
        device = (after, before)[way]
        step = lax.div(i, HALVES)
        return copy(
            block(step, lax.rem(i, HALVES), way, core),
            ring_send.at[way, i], ring_recv.at[way, i], device,
        )

    def arrival(i, way):
        step = lax.div(i, HALVES) + 1
        return copy(
            block(step, lax.rem(i, HALVES), way, core),
            ring_send.at[way, i], ring_recv.at[way, i], (after, before)[way],
        )

    def cross_out(i):
        step = lax.div(i, HALVES) + 1
        return copy(
            block(step, lax.rem(i, HALVES), 0, core),
            ring_send.at[2, i], ring_recv.at[2, i], partner,
        )

    def cross_in(i):
        step = lax.div(i, HALVES) + 1
        return copy(
            block(step, lax.rem(i, HALVES), 2, core),
            ring_send.at[2, i], ring_recv.at[2, i], partner,
        )

    def to_sibling(i, way, of_core):
        step = lax.div(i, HALVES) + 1
        return copy(
            block(step, lax.rem(i, HALVES), way, of_core),
            sib_send.at[way, i], sib_recv.at[way, i], sibling,
        )

    def own_to_sibling(of_core):
        start = pl.multiple_of((2 * chip + of_core) * shard, shard)
        return copy(w.at[pl.ds(start, shard)], own_sem.at[0], own_sem.at[1], sibling)

    loads[0].wait()
    for i in range(HALVES):
        ring(i, 0).start()
        ring(i, 1).start()
    own_to_sibling(core).start()

    def scatter(which, stage, land, peer, source):
        return pltpu.make_async_remote_copy(
            src_ref=stage.at[peer], dst_ref=land.at[source],
            send_sem=rs_send.at[which, peer], recv_sem=rs_recv.at[which, source],
            device_id={"blk": peer}, device_id_type=MESH,
        )

    def spread(which, full, peer, source):
        return pltpu.make_async_remote_copy(
            src_ref=full.at[source], dst_ref=full.at[source],
            send_sem=ag_send.at[which, peer], recv_sem=ag_recv.at[which, source],
            device_id={"blk": peer}, device_id_type=MESH,
        )

    def each_peer(do):
        def body(d, carry):
            do(lax.rem(me + d, blk))
            return carry

        lax.fori_loop(1, blk, body, 0)

    def sum_begin(which, values, stage, land):
        for p in range(blk):
            lat = (p // COLUMN_BLOCKS) * lat_rows
            col = (p % COLUMN_BLOCKS) * mod_cols
            stage[p] = values[lat : lat + lat_rows, col : col + mod_cols]
        each_peer(lambda peer: scatter(which, stage, land, peer, me).start())

    def sum_middle(which, stage, land, full):
        each_peer(lambda peer: scatter(which, stage, land, peer, peer).wait_recv())

        def add(d, value):
            return value + land[lax.rem(me + d, blk)]

        full[me] = lax.fori_loop(1, blk, add, stage[me])
        each_peer(lambda peer: spread(which, full, peer, me).start())

    def sum_end(which, stage, land, full, put):
        each_peer(lambda peer: spread(which, full, peer, peer).wait_recv())
        for p in range(blk):
            lat = (p // COLUMN_BLOCKS) * lat_rows
            col = (p % COLUMN_BLOCKS) * mod_cols
            for r in range(lat_rows):
                put(lat + r, col, full[p, r : r + 1, :])
        each_peer(lambda peer: scatter(which, stage, land, peer, me).wait_send())
        each_peer(lambda peer: spread(which, full, peer, me).wait_send())

    loads[1].wait()
    if overlapped:
        near = cond[:, pl.ds(pl.multiple_of(chip * chip_rows, chip_rows), chip_rows)].astype(F32)
        v = jnp.where(core == 0, near[:, :shard], near[:, shard:])
    else:
        v = cond[...]
    own[...] = v
    act = (v * jax.nn.sigmoid(v)).astype(BF16)
    sum_begin(0, jnp.dot(act, modw[...], preferred_element_type=F32), stage_a, land_a)

    acc[...] = jnp.zeros_like(acc)
    loads[2].wait()

    def multiply(step, way):
        if not overlapped:
            return
        owner = chip_at(place + signs[way] * step)
        k = pl.ds(pl.multiple_of(owner * chip_rows, chip_rows), chip_rows)
        wide = third // 2

        @pl.loop(0, 2)
        def _(n):
            c = pl.ds(pl.multiple_of(cols[way] + n * wide, wide), wide)
            acc[:, c] += jnp.dot(att[:, k], w[k, c], preferred_element_type=F32)

    def from_sibling(step, way):
        for h in range(HALVES):
            to_sibling((step - 1) * HALVES + h, way, 1 - core).wait_recv()

    def put_mod(lat, col, values):
        mod[lat, :, pl.ds(col, mod_cols)] = values

    def turn(i, carry):
        step = lax.div(i, HALVES)
        half = lax.rem(i, HALVES)
        for way in range(2):
            arrival(i, way).wait_recv()

            @pl.when(i + HALVES < total)
            def _(way=way):
                ring(i + HALVES, way).start()

            if way == 0:
                cross_out(i).start()
            to_sibling(i, way, core).start()

        @pl.when(i >= 1)
        def _():
            cross_in(i - 1).wait_recv()
            to_sibling(i - 1, 2, core).start()

        @pl.when(i == 0)
        def _():
            own_to_sibling(1 - core).wait_recv()

        @pl.when(half == 0)
        def _():
            @pl.when(step >= 1)
            def _():
                from_sibling(step, 0)
                from_sibling(step, 1)

            multiply(step, 0)
            multiply(step, 1)

        @pl.when(half == HALVES - 1)
        def _():
            @pl.when(step >= 1)
            def _():
                from_sibling(step, 2)

            multiply(step, 2)

        @pl.when(i == 2 * HALVES)
        def _():
            sum_middle(0, stage_a, land_a, full_a)

        @pl.when(i == 4 * HALVES)
        def _():
            sum_end(0, stage_a, land_a, full_a, put_mod)

        return carry

    lax.fori_loop(0, total, turn, 0)
    from_sibling(steps, 0)
    multiply(steps, 0)
    from_sibling(steps, 1)
    multiply(steps, 1)
    cross_in(total - 1).wait_recv()
    to_sibling(total - 1, 2, core).start()
    from_sibling(steps, 2)
    multiply(steps, 2)

    if not overlapped:
        @pl.loop(0, features // 256)
        def _(n):
            c = pl.ds(pl.multiple_of(n * 256, 256), 256)
            acc[:, c] = jnp.dot(att[...], w[:, c], preferred_element_type=F32)

    for load in loads[3:]:
        load.wait()
    mgrad[...] = jnp.zeros_like(mgrad)
    chunks = features // 128

    def norm(t, carry):
        lat = lax.div(t * TILE, tokens)
        r = pl.ds(pl.multiple_of(t * TILE, TILE), TILE)

        def parts(j):
            c = pl.ds(j * 128, 128)
            gate = mod[lat, :, pl.ds(j * 128, 128)]
            scale = 1.0 + mod[lat, :, pl.ds(2 * features + j * 128, 128)]
            proj = acc[r, c]
            summed = res[r, c].astype(F32) + gate * proj
            cot = ncot[r, c].astype(F32)
            return c, gate, scale, proj, summed, cot

        zero = jnp.zeros((TILE, 128), F32)
        one, two = zero, zero
        for j in range(chunks):
            _, _, scale, _, summed, cot = parts(j)
            one += summed
            two += cot * scale
        average = jnp.sum(one, axis=1, keepdims=True) / features
        grad_mean = jnp.sum(two, axis=1, keepdims=True) / features
        one, two = zero, zero
        for j in range(chunks):
            _, _, scale, _, summed, cot = parts(j)
            centered = summed - average
            one += centered * centered
            two += cot * scale * centered
        inverse = lax.rsqrt(jnp.sum(one, axis=1, keepdims=True) / features + norm_eps)
        grad_norm = inverse * (jnp.sum(two, axis=1, keepdims=True) / features)
        for j in range(chunks):
            c, gate, scale, proj, summed, cot = parts(j)
            normed = (summed - average) * inverse
            shift = mod[lat, :, pl.ds(features + j * 128, 128)]
            grad = rcot[r, c].astype(F32) + inverse * (
                cot * scale - grad_mean - normed * grad_norm
            )
            res[r, c] = (scale * normed + shift).astype(BF16)
            rcot[r, c] = grad.astype(BF16)
            att[r, c] = (grad * gate).astype(BF16)

            def fold_rows(value):
                return jnp.sum(value.reshape(TILE // 8, 8, 128), axis=0)

            for b, value in enumerate((grad * proj, cot, cot * normed)):
                mgrad[lat, :, pl.ds(b * features + j * 128, 128)] += fold_rows(value)
        return carry

    lax.fori_loop(0, rows // TILE, norm, 0)

    sum_begin(1, jnp.sum(mgrad[...], axis=1), stage_b, land_b)

    tiles = 8
    width = features // tiles

    def back(n, carry):
        k = pl.ds(pl.multiple_of(n * width, width), width)
        ncot[:, k] = lax.dot_general(
            att[...], w[k, :], (((1,), (1,)), ((), ())), preferred_element_type=F32
        ).astype(BF16)

        @pl.when(n == 2)
        def _():
            sum_middle(1, stage_b, land_b, full_b)

        return carry

    lax.fori_loop(0, tiles, back, 0)

    def put_grad(lat, col, values):
        grads[lat, :, pl.ds(col, mod_cols)] = values

    sum_end(1, stage_b, land_b, full_b, put_grad)

    def finish(i, carry):
        ring(i, 0).wait_send()
        ring(i, 1).wait_send()
        cross_out(i).wait_send()
        for way in range(3):
            to_sibling(i, way, core).wait_send()
        return carry

    lax.fori_loop(0, total, finish, 0)
    own_to_sibling(core).wait_send()

def finish_kernel(
    latents, seq_len, res, rcot, ncot, grads, cond, modw,
    nout_hbm, rgrad_hbm, agrad_hbm, cgrad, store_sem,
):
    rows = res.shape[0]
    part = rows // STORES
    stores = []
    for a, (src, dst) in enumerate(((res, nout_hbm), (rcot, rgrad_hbm), (ncot, agrad_hbm))):
        for i in range(STORES):
            r = pl.ds(i * part, part)
            stores.append(
                pltpu.make_async_copy(src.at[r], dst.at[r], store_sem.at[a * STORES + i])
            )
    for store in stores:
        store.start()
    total = jnp.concatenate([grads[i] for i in range(latents)], axis=0)
    upper = total.astype(BF16).astype(F32)
    both = jnp.concatenate([upper, total - upper], axis=0).astype(BF16)
    product = lax.dot_general(
        both, modw[...], (((1,), (1,)), ((), ())), preferred_element_type=F32
    )
    v = cond[...]
    gate = jax.nn.sigmoid(v)
    slope = gate * (1.0 + v * (1.0 - gate))
    cgrad[...] = slope * (product[:latents] + product[latents:]) / math.sqrt(seq_len)
    for store in stores:
        store.wait()


def local(groups, blk, residual, attention, condition, proj_weight, mod_weight, residual_cot, normed_cot):
    latents, tokens, features = residual.shape
    rows = latents * tokens
    shard = proj_weight.shape[0]
    pieces = (blk // 2 - 1) * HALVES
    if 2 * shard % 128:
        condition = lax.dynamic_slice_in_dim(
            condition, lax.axis_index("blk") * shard, shard, 1
        ).astype(F32)
    lat_rows = latents * COLUMN_BLOCKS // blk
    mod_cols = 3 * features // COLUMN_BLOCKS
    flat = lambda a: a.reshape(rows, features)
    big = jax.ShapeDtypeStruct((rows, features), BF16)
    held = pltpu.VMEM((rows, features), BF16)
    anywhere = pl.BlockSpec(memory_space=pl.ANY)
    vmem = pl.BlockSpec(memory_space=pltpu.VMEM)
    small = pltpu.VMEM((blk, lat_rows, mod_cols), F32)
    wide = pltpu.VMEM((rows, features), BF16)
    dma = pltpu.SemaphoreType.DMA
    held_outs = pl.pallas_call(
        functools.partial(kernel, groups, blk, latents, tokens),
        out_shape=(held, held, held, pltpu.VMEM((latents, 1, 3 * features), F32),
            pltpu.VMEM((latents, shard), F32)),
        in_specs=[anywhere, anywhere, vmem, anywhere, anywhere, anywhere, anywhere],
        out_specs=(vmem,) * 5,
        scratch_shapes=[
            pltpu.VMEM((shard * blk, features), BF16),
            wide,
            pltpu.VMEM((shard, 3 * features), BF16),
            pltpu.VMEM((rows, features), F32),
            pltpu.VMEM((latents, 1, 3 * features), F32),
            pltpu.VMEM((latents, 8, 3 * features), F32),
            small, small, small, small, small, small,
            dma((6,)),
            dma((3, pieces)), dma((3, pieces)), dma((3, pieces)), dma((3, pieces)),
            dma((2,)),
            dma((2, blk)), dma((2, blk)), dma((2, blk)), dma((2, blk)),
        ],
        compiler_params=pltpu.CompilerParams(
            collective_id=0, has_side_effects=True, vmem_limit_bytes=48 * 2**20
        ),
        cost_estimate=pl.CostEstimate(
            flops=4 * rows * features * features, bytes_accessed=30 * 2**20, transcendentals=0
        ),
    )(
        flat(residual), flat(attention), condition, proj_weight, mod_weight,
        flat(residual_cot), flat(normed_cot),
    )
    outs = pl.pallas_call(
        functools.partial(finish_kernel, latents, tokens * blk),
        out_shape=(big, big, big, jax.ShapeDtypeStruct((latents, shard), F32)),
        in_specs=[vmem] * 6,
        out_specs=(anywhere, anywhere, anywhere, vmem),
        scratch_shapes=[dma((3 * STORES,))],
        compiler_params=pltpu.CompilerParams(vmem_limit_bytes=16 * 2**20),
    )(*held_outs, mod_weight)
    return tuple(a.reshape(latents, tokens, features) for a in outs[:3]) + (outs[3],)


def solution(mesh):
    in_specs = (
        P("groups", "blk", None),
        P("groups", "blk", None),
        P("groups", None),
        P("blk", None),
        P("blk", None),
        P("groups", "blk", None),
        P("groups", "blk", None),
    )
    out_specs = (
        P("groups", "blk", None),
        P("groups", "blk", None),
        P("groups", "blk", None),
        P("groups", "blk"),
    )
    body = functools.partial(local, mesh.shape["groups"], mesh.shape["blk"])
    return jax.shard_map(body, mesh=mesh, in_specs=in_specs, out_specs=out_specs, check_vma=False)
```
